32 devices in a mesh: build: 8 (over y, x, core), lat: 4 (over z).
Axes of the slice: x: 2, y: 2, z: 4, core: 2. Of those that a mesh axis runs over, the one named last changes fastest.
Arguments:
- density: float32 [16, 64, 1024], P('build', 'lat'), may hold values from 0.03 to 1
- support_mask: int32 [64, 1024], P('lat'), may hold values from 0 to 1
- pattern: int32 [27], replicated, may hold values from 0 to 7
- blocks: float32 [8, 3, 3], replicated, may hold values from -0.625 to 0.625
- displacement: float32 [3, 16, 64, 1024], P(None, 'build', 'lat'), may hold values from -6 to 6
- adjoint: float32 [3, 16, 64, 1024], P(None, 'build', 'lat'), may hold values from -6 to 6
Outputs:
- force: float32 [3, 16, 64, 1024], P(None, 'build', 'lat')
- sensitivity: float32 [16, 64, 1024], P('build', 'lat')
The draws below stay inside these ranges and needn't reach their ends.
All inputs are finite; a program needn't handle non-finite values.
Results may differ from the reference program's by a relative error of at most 0.0003.
Values sent between devices are 32-bit elements; how exact they have to be, the bound alone decides.
A program may use at most 64 MiB of HBM per device.

```python
import jax
import jax.numpy as jnp
from jax import lax

CX = 16
NY = 1024
NB = 8
NZ = 16
NX = 64


def draw_density(key, part):
    phase_key = jax.random.fold_in(key, 101)
    lower_key = jax.random.fold_in(key, 202)
    upper_key = jax.random.fold_in(key, 303)
    phase = jax.random.randint(phase_key, (), 0, 2)
    layers = jnp.arange(NZ, dtype=jnp.int32)[:, None, None]
    rows = jnp.arange(NX, dtype=jnp.int32)[None, :, None]
    open_cells = ((layers + rows + phase) % 2 == 1).astype(jnp.float32)
    lower_draw = jax.random.uniform(lower_key, (NZ, NX, NY), jnp.float32)
    upper_draw = jax.random.uniform(upper_key, (NZ, NX, NY), jnp.float32)
    lower_values = 0.03 + 0.02 * lower_draw
    upper_values = 0.65 + 0.35 * upper_draw
    return open_cells * upper_values + (1.0 - open_cells) * lower_values


def draw_support_mask(key, part):
    period = CX * ((2 * NZ + 2 * CX - 3) // CX)
    rows = jnp.arange(NX, dtype=jnp.int32)
    rail = ((rows + NZ - 1) % period == 0) | (rows == NX - 1)
    coverage = jax.random.randint(jax.random.fold_in(key, 404), (NX, NY), 0, 4)
    return (rail[:, None] & (coverage > 0)).astype(jnp.int32)


def set_ends(values, stream_key, smallest, largest):
    dims = values.shape
    spot = [jax.random.randint(jax.random.fold_in(stream_key, axis), (), 0, dims[axis]) for axis in range(len(dims))]
    values = values.at[tuple(spot)].set(smallest)
    longest = dims.index(max(dims))
    spot[longest] = (spot[longest] + 1) % dims[longest]
    return values.at[tuple(spot)].set(largest)


def block_levels(rng, extent, split, smallest, high):
    def one(dim, parts):
        draws = jax.random.uniform(jax.random.fold_in(jax.random.fold_in(rng, 6), dim), (parts,), jnp.float32, smallest / len(split), high / len(split))
        return jnp.repeat(jnp.exp(draws), extent[dim] // parts).reshape((-1,) + (1,) * (len(extent) - dim - 1))

    gain = one(*split[0])
    for cut in split[1:]:
        gain = gain * one(*cut)
    return gain


def centred(key, dims, deviation, bound, pieces=(), kind=jnp.bfloat16):
    drawn = jax.random.normal(key, dims, jnp.float32) * deviation
    if len(pieces) > 0:
        drawn = block_levels(key, dims, pieces, -0.22, 0.18) * drawn
    return jnp.clip(drawn, min=-bound, max=bound).astype(kind)


def setup_inputs(seed: int = 0) -> dict:
    streams_of = jax.random.split(jax.random.key(seed), 7)
    density = draw_density(jax.random.fold_in(streams_of[6], 71), 0)
    support_mask = draw_support_mask(jax.random.fold_in(streams_of[6], 71), 0)
    pattern = set_ends(jax.random.randint(streams_of[2], (27,), 0, NB), jax.random.fold_in(streams_of[2], 1), 0, NB - 1).astype(jnp.int32)
    blocks = centred(streams_of[3], (NB, 3, 3), 81 ** -0.5, 0.625, (), jnp.float32)
    displacement = centred(streams_of[4], (3, NZ, NX, NY), 1.0, 6.0, ((1, 8), (2, 4)), jnp.float32)
    adjoint = centred(streams_of[5], (3, NZ, NX, NY), 1.0, 6.0, ((1, 8), (2, 4)), jnp.float32)
    return dict(density=density, support_mask=support_mask, pattern=pattern, blocks=blocks, displacement=displacement, adjoint=adjoint)


exponent = 16.0
smooth_eps = 0.0001
root_eps = 0.01
base_floor = 0.05
modulus_floor = 0.001
highest = lax.Precision.HIGHEST

def cross_sum(layer_plane):
    padded = jnp.pad(layer_plane, 1)
    centre = padded[1:-1, 1:-1]
    return centre + padded[:-2, 1:-1] + padded[2:, 1:-1] + padded[1:-1, :-2] + padded[1:-1, 2:]

def stencil(values_in, blocks_used, reverse):
    padded = jnp.pad(values_in, ((0, 0), (1, 1), (1, 1), (1, 1)))
    layer_count, width_x, width_y = values_in.shape[1:]
    result = jnp.zeros(values_in.shape, jnp.float32)
    direction = -1 if reverse else 1
    number = 0
    for step_z in (-1, 0, 1):
        for step_x in (-1, 0, 1):
            for step_y in (-1, 0, 1):
                start_z = 1 + direction * step_z
                start_x = 1 + direction * step_x
                start_y = 1 + direction * step_y
                shifted = padded[:, start_z:start_z + layer_count, start_x:start_x + width_x, start_y:start_y + width_y]
                matrix = blocks_used[number].T if reverse else blocks_used[number]
                result = result + jnp.einsum('cd,dzxy->czxy', matrix, shifted, precision=highest)
                number += 1
    return result

def reference(density, support_mask, pattern, blocks, displacement, adjoint):
    base_plane = base_floor + (1.0 - base_floor) * support_mask.astype(jnp.float32)

    def forward_layer(from_below, design_layer):
        support = cross_sum(from_below ** exponent) ** (1.0 / exponent)
        differ = design_layer - support
        printed = 0.5 * (design_layer + support - jnp.sqrt(differ * differ + smooth_eps) + root_eps)
        return (printed, (printed, support))
    _, (printed, support) = lax.scan(forward_layer, base_plane, density)
    modulus = modulus_floor + (1.0 - modulus_floor) * printed ** 3
    blocks_used = blocks[pattern]
    force = stencil(modulus[None] * displacement, blocks_used, False)
    pulled = stencil(adjoint, blocks_used, True)
    direct = lax.optimization_barrier(jnp.sum(displacement * pulled, axis=0)) * (3.0 * (1.0 - modulus_floor)) * printed ** 2

    def backward_layer(from_above, layer_items):
        direct_layer, printed_layer, support_layer, design_layer = layer_items
        weight_total = direct_layer + printed_layer ** (exponent - 1.0) * cross_sum(from_above)
        differ = design_layer - support_layer
        slope_term = differ / jnp.sqrt(differ * differ + smooth_eps)
        sensitivity = weight_total * 0.5 * (1.0 - slope_term)
        passed = weight_total * 0.5 * (1.0 + slope_term) / support_layer ** (exponent - 1.0)
        return (passed, sensitivity)
    zero_plane = jnp.zeros(density.shape[1:], jnp.float32)
    _, sensitivity = lax.scan(backward_layer, zero_plane, (direct, printed, support, density), reverse=True)
    return (force, sensitivity)
```

```python
import functools

import jax
import jax.numpy as jnp
import numpy as np
from jax import lax
from jax.experimental import pallas as pl
from jax.experimental.pallas import tpu as pltpu
from jax.sharding import PartitionSpec as P

smooth_eps = 0.0001
root_eps = 0.01
base_floor = 0.05
modulus_floor = 0.001
HALO = 8
MESH = pl.DeviceIdType.MESH
COPIES = 23
NO_KEY = 1 << 20


def lane_keys(layers, rows, first_field):
    deep = layers + 2
    inner = 3 * deep * rows
    total = inner + 2 * deep * HALO
    place = np.full((2, total), NO_KEY, np.int32)
    for k in range(total):
        if k < inner:
            place[0, k] = k // rows
            place[1, k] = k % rows
        else:
            e = k - inner
            side, z, f = e // (deep * HALO), (e // HALO) % deep, e % HALO - first_field
            if 0 <= f < 3:
                place[0, k] = f * deep + z
                place[1, k] = -1 if side == 0 else rows
    return place


def kernel(
    nb, nlat,
    pattern, blocks, keys, den, smask, disp, adj,
    force, sens,
    dext, rin, pext, sext, above, cbin, pas, base, coef, gext, dz, az, es, er,
    mats, xs, prod, send_sem, recv_sem,
):
    nl, nx, ny = den.shape
    rows = nx + 2 * HALO
    deep = nl + 2
    mid = slice(HALO, HALO + nx)
    lo = slice(0, HALO)
    hi = slice(HALO + nx, rows)
    b = lax.axis_index("build")
    l = lax.axis_index("lat")
    first_b, last_b = b == 0, b == nb - 1
    upper = b >= nb // 2

    top = nl - 1
    table = [
        (lambda: den.at[:, nx - HALO : nx], lambda: dext.at[:, lo], 0, 1),
        (lambda: den.at[:, 0:HALO], lambda: dext.at[:, hi], 0, -1),
        (lambda: es.at[1], lambda: er.at[0, 1 : 1 + nl], 0, 1),
        (lambda: es.at[0], lambda: er.at[1, 1 : 1 + nl], 0, -1),
        (lambda: es.at[1, top], lambda: er.at[0, 0], 1, 1),
        (lambda: es.at[0, top], lambda: er.at[1, 0], 1, -1),
        (lambda: es.at[1, 0], lambda: er.at[0, nl + 1], -1, 1),
        (lambda: es.at[0, 0], lambda: er.at[1, nl + 1], -1, -1),
        (lambda: adj.at[:, top], lambda: az.at[0], 1, 0),
        (lambda: adj.at[:, 0], lambda: az.at[1], -1, 0),
        (lambda: disp.at[:, top], lambda: dz.at[0], 1, 0),
        (lambda: disp.at[:, 0], lambda: dz.at[1], -1, 0),
        (lambda: pext.at[top, mid], lambda: rin.at[mid], 1, 0),
        (lambda: pext.at[top, nx : nx + HALO], lambda: rin.at[lo], 1, 1),
        (lambda: pext.at[top, HALO : 2 * HALO], lambda: rin.at[hi], 1, -1),
        (lambda: base.at[nx - HALO : nx], lambda: rin.at[lo], 0, 1),
        (lambda: base.at[0:HALO], lambda: rin.at[hi], 0, -1),
        (lambda: pext.at[0], lambda: above, -1, 0),
        (lambda: gext.at[:, nx : nx + HALO], lambda: gext.at[:, lo], 0, 1),
        (lambda: gext.at[:, HALO : 2 * HALO], lambda: gext.at[:, hi], 0, -1),
        (lambda: pas.at[0:nx], lambda: cbin.at[mid], -1, 0),
        (lambda: pas.at[nx - HALO : nx], lambda: cbin.at[lo], -1, 1),
        (lambda: pas.at[0:HALO], lambda: cbin.at[hi], -1, -1),
    ]

    def there(db, dl):
        ok = None
        for at, step, count in ((b, db, nb), (l, dl, nlat)):
            if step == 0:
                continue
            here = at < count - 1 if step > 0 else at > 0
            ok = here if ok is None else jnp.logical_and(ok, here)
        return ok

    def may_send(i):
        _, _, db, dl = table[i]
        ok = there(db, dl)
        return jnp.logical_and(ok, first_b) if i in (15, 16) else ok

    def may_take(i):
        _, _, db, dl = table[i]
        ok = there(-db, -dl)
        return jnp.logical_and(ok, first_b) if i in (15, 16) else ok

    def made(i):
        src, dst, db, dl = table[i]
        return pltpu.make_async_remote_copy(
            src_ref=src(), dst_ref=dst(),
            send_sem=send_sem.at[i], recv_sem=recv_sem.at[i],
            device_id=(b + db, l + dl), device_id_type=MESH,
        )

    def start(*numbers):
        for i in numbers:
            @pl.when(may_send(i))
            def _():
                made(i).start()

    def take(*numbers):
        for i in numbers:
            @pl.when(may_take(i))
            def _():
                made(i).wait_recv()

    def zero_if(cond, ref):
        @pl.when(cond)
        def _():
            ref[...] = jnp.zeros(ref.shape, jnp.float32)

    row_at = l * nx - HALO + lax.broadcasted_iota(jnp.int32, (rows, ny), 0)
    inside = jnp.logical_and(row_at >= 0, row_at < nlat * nx)

    def beside(w):
        col = lax.broadcasted_iota(jnp.int32, w.shape, 1)
        left = jnp.where(col == 0, 0.0, pltpu.roll(w, 1, 1))
        right = jnp.where(col == ny - 1, 0.0, pltpu.roll(w, ny - 1, 1))
        return left, right

    def cross(w):
        left, right = beside(w)
        return w + pltpu.roll(w, 1, 0) + pltpu.roll(w, rows - 1, 0) + left + right

    barrier = pltpu.get_barrier_semaphore()
    steps = [(i, j) for i in (-1, 0, 1) for j in (-1, 0, 1) if (i, j) != (0, 0)]
    for i, j in steps:
        @pl.when(there(i, j))
        def _():
            pl.semaphore_signal(barrier, inc=1, device_id=(b + i, l + j), device_id_type=MESH)
    wide = 1 + (b > 0).astype(jnp.int32) + (b < nb - 1).astype(jnp.int32)
    tall = 1 + (l > 0).astype(jnp.int32) + (l < nlat - 1).astype(jnp.int32)
    pl.semaphore_wait(barrier, wide * tall - 1)

    start(0, 1)

    @pl.when(first_b)
    def _():
        plane = base_floor + (1.0 - base_floor) * smask[...].astype(jnp.float32)
        base[...] = plane
        rin[mid] = plane

    start(15, 16)
    for z in range(nl):
        dext[z, mid] = den[z]
    for side, row in ((0, 0), (1, nx - 1)):
        for z in range(nl):
            for d in range(3):
                es[side, z, d : d + 1, :] = disp[d, z, row : row + 1, :]
                es[side, z, 3 + d : 4 + d, :] = adj[d, z, row : row + 1, :]
            es[side, z, 6:8, :] = jnp.zeros((2, ny), jnp.float32)
    start(2, 3, 4, 5, 6, 7, 8, 9)

    for i in (0, 1, 2, 3, 4, 5, 6, 7, 8, 9, 10, 11, 17, 18, 19, 20):
        _, dst, db, dl = table[i]
        zero_if(jnp.logical_not(there(-db, -dl)), dst())
    zero_if(l == 0, rin.at[lo])
    zero_if(l == nlat - 1, rin.at[hi])
    zero_if(jnp.logical_or(last_b, l == 0), cbin.at[lo])
    zero_if(jnp.logical_or(last_b, l == nlat - 1), cbin.at[hi])

    def forward():
        take(0, 1, 12, 13, 14, 15, 16)
        p = rin[...]
        for z in range(nl):
            p2 = p * p
            p4 = p2 * p2
            p8 = p4 * p4
            w = jnp.where(inside, p8 * p8, 0.0)
            total = jnp.where(inside, cross(w), 1.0)
            s = lax.rsqrt(lax.rsqrt(lax.rsqrt(lax.rsqrt(total))))
            d = dext[z]
            differ = d - s
            t = differ * differ + smooth_eps
            p = 0.5 * (d + s - t * lax.rsqrt(t) + root_eps)
            pext[z] = p
            sext[z] = s
        start(12, 13, 14, 17, 10, 11)
        for z in range(nl):
            p, s, d = pext[z], sext[z], dext[z]
            differ = d - s
            slope = differ * lax.rsqrt(differ * differ + smooth_eps)
            p2 = p * p
            p4 = p2 * p2
            p8 = p4 * p4
            s2 = s * s
            s4 = s2 * s2
            s8 = s4 * s4
            coef[0, z] = p8 * p4 * (p2 * p)
            coef[1, z] = jnp.where(inside, 0.5 * (1.0 + slope) / (s8 * s4 * (s2 * s)), 0.0)
            coef[2, z] = 0.5 * (1.0 - slope)
            coef[3, z] = (3.0 * (1.0 - modulus_floor)) * p2

    wide_k = keys.shape[-1]

    def build(which):
        x = lax.broadcasted_iota(jnp.int32, (nx, wide_k), 0)
        dzk = jnp.broadcast_to(keys[which, 0:1, :], (nx, wide_k))
        off = jnp.broadcast_to(keys[which, 1:2, :], (nx, wide_k)) - x + 1
        near = jnp.logical_and(off >= 0, off <= 2)
        key = jnp.where(near, dzk * 4 + off, -1)
        for z in range(nl):
            for c in range(3):
                sums = [jnp.zeros((nx, wide_k), jnp.float32) for _ in range(3)]
                for d in range(3):
                    for a in range(3):
                        for bx in range(3):
                            hit = key == (d * deep + z + a) * 4 + bx
                            for s in range(3):
                                o = 9 * a + 3 * bx + s
                                if which == 0:
                                    value = blocks[pattern[o], c, d]
                                else:
                                    value = blocks[pattern[26 - o], d, c]
                                sums[s] = jnp.where(hit, value, sums[s])
                for s in range(3):
                    at = ((s * 3 + c) * nl + z) * nx
                    high = sums[s].astype(jnp.bfloat16)
                    mats[0, at : at + nx, :] = high
                    mats[1, at : at + nx, :] = (sums[s] - high.astype(jnp.float32)).astype(
                        jnp.bfloat16
                    )

    def multiply():
        step = 256 if ny % 256 == 0 else 128

        def chunk(n, _):
            cols = pl.ds(pl.multiple_of(n * step, step), step)
            x = xs[:, cols]
            xh = x.astype(jnp.bfloat16)
            xl = (x - xh.astype(jnp.float32)).astype(jnp.bfloat16)
            dot = functools.partial(jnp.dot, preferred_element_type=jnp.float32)
            prod[:, cols] = dot(mats[0], xh) + (dot(mats[0], xl) + dot(mats[1], xh))
            return 0

        lax.fori_loop(0, ny // step, chunk, 0)

    def gathered(c):
        n = nl * nx
        left, _ = beside(prod[c * n : (c + 1) * n, :])
        _, right = beside(prod[(6 + c) * n : (7 + c) * n, :])
        return prod[(3 + c) * n : (4 + c) * n, :] + left + right

    inner = 3 * deep * nx

    def early():
        build(1)
        take(2, 3, 4, 5, 6, 7, 8, 9)
        for d in range(3):
            for z in range(deep):
                at = (d * deep + z) * nx
                if z == 0:
                    xs[at : at + nx, :] = az[0, d]
                elif z == deep - 1:
                    xs[at : at + nx, :] = az[1, d]
                else:
                    xs[at : at + nx, :] = adj[d, z - 1]
        for side in range(2):
            for z in range(deep):
                at = inner + (side * deep + z) * HALO
                xs[at : at + HALO, :] = er[side, z]
        multiply()
        parts = [gathered(c) for c in range(3)]
        for z in range(nl):
            g = disp[0, z] * parts[0][z * nx : (z + 1) * nx]
            g = g + disp[1, z] * parts[1][z * nx : (z + 1) * nx]
            gext[z, mid] = g + disp[2, z] * parts[2][z * nx : (z + 1) * nx]
        start(18, 19)
        build(0)

    def first(i, _):
        turn = (i == 0) == upper
        pl.when(turn)(early)
        pl.when(jnp.logical_not(turn))(forward)
        return 0

    lax.fori_loop(0, 2, first, 0)

    take(18, 19)
    for z in range(nl):
        coef[3, z] = coef[3, z] * gext[z]

    def stiffness():
        take(10, 11, 17)
        for z in range(deep):
            ref = rin if z == 0 else (above if z == deep - 1 else pext.at[z - 1])
            p = ref[mid]
            m = modulus_floor + (1.0 - modulus_floor) * (p * p * p)
            for d in range(3):
                at = (d * deep + z) * nx
                if z == 0:
                    u = dz[0, d]
                elif z == deep - 1:
                    u = dz[1, d]
                else:
                    u = disp[d, z - 1]
                xs[at : at + nx, :] = m * u
            for side, row in ((0, HALO - 1), (1, HALO + nx)):
                at = inner + (side * deep + z) * HALO
                p = ref[row : row + 1, :]
                m = modulus_floor + (1.0 - modulus_floor) * (p * p * p)
                xs[at : at + HALO, :] = m * er[side, z]
        multiply()
        for c in range(3):
            part = gathered(c)
            for z in range(nl):
                force[c, z] = part[z * nx : (z + 1) * nx]

    def backward():
        take(20, 21, 22)
        passed = cbin[...]
        for z in reversed(range(nl)):
            total = coef[3, z] + coef[0, z] * cross(passed)
            passed = total * coef[1, z]
            if z == 0:
                pas[...] = passed[HALO : HALO + nx]
                start(20, 21, 22)
            sens[z] = (total * coef[2, z])[HALO : HALO + nx]

    def second(i, _):
        turn = (i == 0) == upper
        pl.when(turn)(backward)
        pl.when(jnp.logical_not(turn))(stiffness)
        return 0

    lax.fori_loop(0, 2, second, 0)

    for i in range(COPIES):
        @pl.when(may_send(i))
        def _():
            made(i).wait_send()


def on_device(density, support_mask, pattern, blocks, displacement, adjoint):
    nb, nlat = lax.axis_size("build"), lax.axis_size("lat")
    nl, nx, ny = density.shape
    rows, deep = nx + 2 * HALO, nl + 2
    keys = np.stack([lane_keys(nl, nx, 0), lane_keys(nl, nx, 3)])
    wide_k = keys.shape[-1]
    f32 = jnp.float32
    vmem = pl.BlockSpec(memory_space=pltpu.VMEM)
    smem = pl.BlockSpec(memory_space=pltpu.SMEM)
    force, sens = pl.pallas_call(
        functools.partial(kernel, nb, nlat),
        out_shape=(
            jax.ShapeDtypeStruct(displacement.shape, f32),
            jax.ShapeDtypeStruct(density.shape, f32),
        ),
        in_specs=[smem, smem, vmem, vmem, vmem, vmem, vmem],
        out_specs=(vmem, vmem),
        scratch_shapes=[
            pltpu.VMEM((nl, rows, ny), f32),
            pltpu.VMEM((rows, ny), f32),
            pltpu.VMEM((nl, rows, ny), f32),
            pltpu.VMEM((nl, rows, ny), f32),
            pltpu.VMEM((rows, ny), f32),
            pltpu.VMEM((rows, ny), f32),
            pltpu.VMEM((nx, ny), f32),
            pltpu.VMEM((nx, ny), f32),
            pltpu.VMEM((4, nl, rows, ny), f32),
            pltpu.VMEM((nl, rows, ny), f32),
            pltpu.VMEM((2, 3, nx, ny), f32),
            pltpu.VMEM((2, 3, nx, ny), f32),
            pltpu.VMEM((2, nl, HALO, ny), f32),
            pltpu.VMEM((2, deep, HALO, ny), f32),
            pltpu.VMEM((2, 9 * nl * nx, wide_k), jnp.bfloat16),
            pltpu.VMEM((wide_k, ny), f32),
            pltpu.VMEM((9 * nl * nx, ny), f32),
            pltpu.SemaphoreType.DMA((COPIES,)),
            pltpu.SemaphoreType.DMA((COPIES,)),
        ],
        compiler_params=pltpu.CompilerParams(
            collective_id=0, has_side_effects=True, vmem_limit_bytes=48 * 1024 * 1024
        ),
    )(pattern, blocks, jnp.asarray(keys), density, support_mask, displacement, adjoint)
    return force, sens


def solution(mesh):
    in_specs = (
        P("build", "lat", None),
        P("lat", None),
        P(),
        P(),
        P(None, "build", "lat", None),
        P(None, "build", "lat", None),
    )
    out_specs = (P(None, "build", "lat", None), P("build", "lat", None))
    return jax.shard_map(
        on_device, mesh=mesh, in_specs=in_specs, out_specs=out_specs, check_vma=False
    )
```

```python
import functools

import jax
import jax.numpy as jnp
import numpy as np
from jax import lax
from jax.experimental import pallas as pl
from jax.experimental.pallas import tpu as pltpu
from jax.sharding import PartitionSpec as P

smooth_eps = 0.0001
root_eps = 0.01
base_floor = 0.05
modulus_floor = 0.001
HALO = 8
MESH = pl.DeviceIdType.MESH
COPIES = 23
NO_KEY = 1 << 20


def lane_keys(layers, rows, first_field):
    deep = layers + 2
    inner = 3 * deep * rows
    total = inner + 2 * deep * HALO
    place = np.full((2, total), NO_KEY, np.int32)
    for k in range(total):
        if k < inner:
            place[0, k] = k // rows
            place[1, k] = k % rows
        else:
            e = k - inner
            side, z, f = e // (deep * HALO), (e // HALO) % deep, e % HALO - first_field
            if 0 <= f < 3:
                place[0, k] = f * deep + z
                place[1, k] = -1 if side == 0 else rows
    return place


def kernel(
    nb, nlat,
    pattern, blocks, keys, den_in, smask_in, disp_in, adj_in,
    force, sens,
    den, smask, disp, adj,
    dext, rin, pext, sext, above, cbin, pas, base, coef, gext, dz, az, es, er,
    mats, xs, prod, send_sem, recv_sem, local_sem,
):
    nl, nx, ny = den.shape
    rows = nx + 2 * HALO
    deep = nl + 2
    mid = slice(HALO, HALO + nx)
    lo = slice(0, HALO)
    hi = slice(HALO + nx, rows)
    b = lax.axis_index("build")
    l = lax.axis_index("lat")
    first_b, last_b = b == 0, b == nb - 1
    upper = b >= nb // 2

    top = nl - 1
    table = [
        (lambda: den.at[:, nx - HALO : nx], lambda: dext.at[:, lo], 0, 1),
        (lambda: den.at[:, 0:HALO], lambda: dext.at[:, hi], 0, -1),
        (lambda: es.at[1], lambda: er.at[0, 1 : 1 + nl], 0, 1),
        (lambda: es.at[0], lambda: er.at[1, 1 : 1 + nl], 0, -1),
        (lambda: es.at[1, top], lambda: er.at[0, 0], 1, 1),
        (lambda: es.at[0, top], lambda: er.at[1, 0], 1, -1),
        (lambda: es.at[1, 0], lambda: er.at[0, nl + 1], -1, 1),
        (lambda: es.at[0, 0], lambda: er.at[1, nl + 1], -1, -1),
        (lambda: adj.at[:, top], lambda: az.at[0], 1, 0),
        (lambda: adj.at[:, 0], lambda: az.at[1], -1, 0),
        (lambda: disp.at[:, top], lambda: dz.at[0], 1, 0),
        (lambda: disp.at[:, 0], lambda: dz.at[1], -1, 0),
        (lambda: pext.at[top, mid], lambda: rin.at[mid], 1, 0),
        (lambda: pext.at[top, nx : nx + HALO], lambda: rin.at[lo], 1, 1),
        (lambda: pext.at[top, HALO : 2 * HALO], lambda: rin.at[hi], 1, -1),
        (lambda: base.at[nx - HALO : nx], lambda: rin.at[lo], 0, 1),
        (lambda: base.at[0:HALO], lambda: rin.at[hi], 0, -1),
        (lambda: pext.at[0], lambda: above, -1, 0),
        (lambda: gext.at[:, nx : nx + HALO], lambda: gext.at[:, lo], 0, 1),
        (lambda: gext.at[:, HALO : 2 * HALO], lambda: gext.at[:, hi], 0, -1),
        (lambda: pas.at[0:nx], lambda: cbin.at[mid], -1, 0),
        (lambda: pas.at[nx - HALO : nx], lambda: cbin.at[lo], -1, 1),
        (lambda: pas.at[0:HALO], lambda: cbin.at[hi], -1, -1),
    ]

    def there(db, dl):
        ok = None
        for at, step, count in ((b, db, nb), (l, dl, nlat)):
            if step == 0:
                continue
            here = at < count - 1 if step > 0 else at > 0
            ok = here if ok is None else jnp.logical_and(ok, here)
        return ok

    def may_send(i):
        _, _, db, dl = table[i]
        ok = there(db, dl)
        return jnp.logical_and(ok, first_b) if i in (15, 16) else ok

    def may_take(i):
        _, _, db, dl = table[i]
        ok = there(-db, -dl)
        return jnp.logical_and(ok, first_b) if i in (15, 16) else ok

    def made(i):
        src, dst, db, dl = table[i]
        return pltpu.make_async_remote_copy(
            src_ref=src(), dst_ref=dst(),
            send_sem=send_sem.at[i], recv_sem=recv_sem.at[i],
            device_id=(b + db, l + dl), device_id_type=MESH,
        )

    def start(*numbers):
        for i in numbers:
            @pl.when(may_send(i))
            def _():
                made(i).start()

    def take(*numbers):
        for i in numbers:
            @pl.when(may_take(i))
            def _():
                made(i).wait_recv()

    def zero_if(cond, ref):
        @pl.when(cond)
        def _():
            ref[...] = jnp.zeros(ref.shape, jnp.float32)

    row_at = l * nx - HALO + lax.broadcasted_iota(jnp.int32, (rows, ny), 0)
    inside = jnp.logical_and(row_at >= 0, row_at < nlat * nx)

    def beside(w):
        col = lax.broadcasted_iota(jnp.int32, w.shape, 1)
        left = jnp.where(col == 0, 0.0, pltpu.roll(w, 1, 1))
        right = jnp.where(col == ny - 1, 0.0, pltpu.roll(w, ny - 1, 1))
        return left, right

    def cross(w):
        left, right = beside(w)
        return w + pltpu.roll(w, 1, 0) + pltpu.roll(w, rows - 1, 0) + left + right

    loads = [
        pltpu.make_async_copy(src, dst, local_sem.at[n])
        for n, (src, dst) in enumerate(
            ((den_in, den), (smask_in, smask), (adj_in, adj), (disp_in, disp))
        )
    ]
    for load in loads:
        load.start()
    barrier = pltpu.get_barrier_semaphore()
    steps = [(i, j) for i in (-1, 0, 1) for j in (-1, 0, 1) if (i, j) != (0, 0)]
    for i, j in steps:
        @pl.when(there(i, j))
        def _():
            pl.semaphore_signal(barrier, inc=1, device_id=(b + i, l + j), device_id_type=MESH)
    wide = 1 + (b > 0).astype(jnp.int32) + (b < nb - 1).astype(jnp.int32)
    tall = 1 + (l > 0).astype(jnp.int32) + (l < nlat - 1).astype(jnp.int32)
    pl.semaphore_wait(barrier, wide * tall - 1)

    loads[0].wait()
    start(0, 1)
    loads[1].wait()

    @pl.when(first_b)
    def _():
        plane = base_floor + (1.0 - base_floor) * smask[...].astype(jnp.float32)
        base[...] = plane
        rin[mid] = plane

    start(15, 16)
    for z in range(nl):
        dext[z, mid] = den[z]
    loads[2].wait()
    loads[3].wait()
    for side, row in ((0, 0), (1, nx - 1)):
        for z in range(nl):
            for d in range(3):
                es[side, z, d : d + 1, :] = disp[d, z, row : row + 1, :]
                es[side, z, 3 + d : 4 + d, :] = adj[d, z, row : row + 1, :]
            es[side, z, 6:8, :] = jnp.zeros((2, ny), jnp.float32)
    start(2, 3, 4, 5, 6, 7, 8, 9)

    @pl.when(upper)
    def _():
        start(10, 11)

    for i in (0, 1, 2, 3, 4, 5, 6, 7, 8, 9, 10, 11, 17, 18, 19, 20):
        _, dst, db, dl = table[i]
        zero_if(jnp.logical_not(there(-db, -dl)), dst())
    zero_if(l == 0, rin.at[lo])
    zero_if(l == nlat - 1, rin.at[hi])
    zero_if(jnp.logical_or(last_b, l == 0), cbin.at[lo])
    zero_if(jnp.logical_or(last_b, l == nlat - 1), cbin.at[hi])

    def forward():
        take(0, 1, 12, 13, 14, 15, 16)
        p = rin[...]
        for z in range(nl):
            p2 = p * p
            p4 = p2 * p2
            p8 = p4 * p4
            w = jnp.where(inside, p8 * p8, 0.0)
            total = jnp.where(inside, cross(w), 1.0)
            s = lax.rsqrt(lax.rsqrt(lax.rsqrt(lax.rsqrt(total))))
            d = dext[z]
            differ = d - s
            t = differ * differ + smooth_eps
            p = 0.5 * (d + s - t * lax.rsqrt(t) + root_eps)
            pext[z] = p
            sext[z] = s
        start(13, 14, 12, 17)
        for z in range(nl):
            p, s, d = pext[z], sext[z], dext[z]
            differ = d - s
            slope = differ * lax.rsqrt(differ * differ + smooth_eps)
            p2 = p * p
            p4 = p2 * p2
            p8 = p4 * p4
            s2 = s * s
            s4 = s2 * s2
            s8 = s4 * s4
            coef[0, z] = p8 * p4 * (p2 * p)
            coef[1, z] = jnp.where(inside, 0.5 * (1.0 + slope) / (s8 * s4 * (s2 * s)), 0.0)
            coef[2, z] = 0.5 * (1.0 - slope)
            coef[3, z] = (3.0 * (1.0 - modulus_floor)) * p2

    wide_k = keys.shape[-1]

    def build(which):
        x = lax.broadcasted_iota(jnp.int32, (nx, wide_k), 0)
        dzk = jnp.broadcast_to(keys[which, 0:1, :], (nx, wide_k))
        off = jnp.broadcast_to(keys[which, 1:2, :], (nx, wide_k)) - x + 1
        near = jnp.logical_and(off >= 0, off <= 2)
        key = jnp.where(near, dzk * 4 + off, -1)
        for z in range(nl):
            for c in range(3):
                sums = [jnp.zeros((nx, wide_k), jnp.float32) for _ in range(3)]
                for d in range(3):
                    for a in range(3):
                        for bx in range(3):
                            hit = key == (d * deep + z + a) * 4 + bx
                            for s in range(3):
                                o = 9 * a + 3 * bx + s
                                if which == 0:
                                    value = blocks[c, d, pattern[o]]
                                else:
                                    value = blocks[d, c, pattern[26 - o]]
                                sums[s] = jnp.where(hit, value, sums[s])
                for s in range(3):
                    at = ((s * 3 + c) * nl + z) * nx
                    high = sums[s].astype(jnp.bfloat16)
                    mats[0, at : at + nx, :] = high
                    mats[1, at : at + nx, :] = (sums[s] - high.astype(jnp.float32)).astype(
                        jnp.bfloat16
                    )

    def multiply():
        step = 256 if ny % 256 == 0 else 128

        def chunk(n, _):
            cols = pl.ds(pl.multiple_of(n * step, step), step)
            x = xs[:, cols]
            xh = x.astype(jnp.bfloat16)
            xl = (x - xh.astype(jnp.float32)).astype(jnp.bfloat16)
            dot = functools.partial(jnp.dot, preferred_element_type=jnp.float32)
            prod[:, cols] = dot(mats[0], xh) + (dot(mats[0], xl) + dot(mats[1], xh))
            return 0

        lax.fori_loop(0, ny // step, chunk, 0)

    def gathered(c):
        n = nl * nx
        left, _ = beside(prod[c * n : (c + 1) * n, :])
        _, right = beside(prod[(6 + c) * n : (7 + c) * n, :])
        return prod[(3 + c) * n : (4 + c) * n, :] + left + right

    inner = 3 * deep * nx

    def early():
        build(1)
        take(2, 3, 4, 5, 6, 7, 8, 9)
        for d in range(3):
            for z in range(deep):
                at = (d * deep + z) * nx
                if z == 0:
                    xs[at : at + nx, :] = az[0, d]
                elif z == deep - 1:
                    xs[at : at + nx, :] = az[1, d]
                else:
                    xs[at : at + nx, :] = adj[d, z - 1]
        for side in range(2):
            for z in range(deep):
                at = inner + (side * deep + z) * HALO
                xs[at : at + HALO, :] = er[side, z]
        multiply()
        parts = [gathered(c) for c in range(3)]
        for z in range(nl):
            g = disp[0, z] * parts[0][z * nx : (z + 1) * nx]
            g = g + disp[1, z] * parts[1][z * nx : (z + 1) * nx]
            gext[z, mid] = g + disp[2, z] * parts[2][z * nx : (z + 1) * nx]
        start(18, 19)
        build(0)

    def first(i, _):
        turn = (i == 0) == upper
        pl.when(turn)(early)
        pl.when(jnp.logical_not(turn))(forward)
        return 0

    lax.fori_loop(0, 2, first, 0)

    @pl.when(jnp.logical_not(upper))
    def _():
        start(10, 11)

    take(18, 19)
    for z in range(nl):
        coef[3, z] = coef[3, z] * gext[z]

    def stiffness():
        take(10, 11, 17)
        for z in range(deep):
            ref = rin if z == 0 else (above if z == deep - 1 else pext.at[z - 1])
            p = ref[mid]
            m = modulus_floor + (1.0 - modulus_floor) * (p * p * p)
            for d in range(3):
                at = (d * deep + z) * nx
                if z == 0:
                    u = dz[0, d]
                elif z == deep - 1:
                    u = dz[1, d]
                else:
                    u = disp[d, z - 1]
                xs[at : at + nx, :] = m * u
            for side, row in ((0, HALO - 1), (1, HALO + nx)):
                at = inner + (side * deep + z) * HALO
                p = ref[row : row + 1, :]
                m = modulus_floor + (1.0 - modulus_floor) * (p * p * p)
                xs[at : at + HALO, :] = m * er[side, z]
        multiply()
        for c in range(3):
            part = gathered(c)
            for z in range(nl):
                force[c, z] = part[z * nx : (z + 1) * nx]

    def backward():
        take(20, 21, 22)
        passed = cbin[...]
        for z in reversed(range(nl)):
            total = coef[3, z] + coef[0, z] * cross(passed)
            passed = total * coef[1, z]
            if z == 0:
                pas[...] = passed[HALO : HALO + nx]
                start(21, 22, 20)
            sens[z] = (total * coef[2, z])[HALO : HALO + nx]

    def second(i, _):
        turn = (i == 0) == upper
        pl.when(turn)(backward)
        pl.when(jnp.logical_not(turn))(stiffness)
        return 0

    lax.fori_loop(0, 2, second, 0)

    for i in range(COPIES):
        @pl.when(may_send(i))
        def _():
            made(i).wait_send()


def on_device(density, support_mask, pattern, blocks, displacement, adjoint):
    nb, nlat = lax.axis_size("build"), lax.axis_size("lat")
    nl, nx, ny = density.shape
    rows, deep = nx + 2 * HALO, nl + 2
    keys = np.stack([lane_keys(nl, nx, 0), lane_keys(nl, nx, 3)])
    wide_k = keys.shape[-1]
    f32 = jnp.float32
    vmem = pl.BlockSpec(memory_space=pltpu.VMEM)
    smem = pl.BlockSpec(memory_space=pltpu.SMEM)
    hbm = pl.BlockSpec(memory_space=pltpu.HBM)
    force, sens = pl.pallas_call(
        functools.partial(kernel, nb, nlat),
        out_shape=(
            jax.ShapeDtypeStruct(displacement.shape, f32),
            jax.ShapeDtypeStruct(density.shape, f32),
        ),
        in_specs=[smem, smem, vmem, hbm, hbm, hbm, hbm],
        out_specs=(vmem, vmem),
        scratch_shapes=[
            pltpu.VMEM(density.shape, f32),
            pltpu.VMEM(support_mask.shape, jnp.int32),
            pltpu.VMEM(displacement.shape, f32),
            pltpu.VMEM(adjoint.shape, f32),
            pltpu.VMEM((nl, rows, ny), f32),
            pltpu.VMEM((rows, ny), f32),
            pltpu.VMEM((nl, rows, ny), f32),
            pltpu.VMEM((nl, rows, ny), f32),
            pltpu.VMEM((rows, ny), f32),
            pltpu.VMEM((rows, ny), f32),
            pltpu.VMEM((nx, ny), f32),
            pltpu.VMEM((nx, ny), f32),
            pltpu.VMEM((4, nl, rows, ny), f32),
            pltpu.VMEM((nl, rows, ny), f32),
            pltpu.VMEM((2, 3, nx, ny), f32),
            pltpu.VMEM((2, 3, nx, ny), f32),
            pltpu.VMEM((2, nl, HALO, ny), f32),
            pltpu.VMEM((2, deep, HALO, ny), f32),
            pltpu.VMEM((2, 9 * nl * nx, wide_k), jnp.bfloat16),
            pltpu.VMEM((wide_k, ny), f32),
            pltpu.VMEM((9 * nl * nx, ny), f32),
            pltpu.SemaphoreType.DMA((COPIES,)),
            pltpu.SemaphoreType.DMA((COPIES,)),
            pltpu.SemaphoreType.DMA((4,)),
        ],
        compiler_params=pltpu.CompilerParams(
            collective_id=0, has_side_effects=True, vmem_limit_bytes=63 * 1024 * 1024
        ),
    )(pattern, jnp.transpose(blocks, (1, 2, 0)), jnp.asarray(keys), density, support_mask, displacement, adjoint)
    return force, sens


def solution(mesh):
    in_specs = (
        P("build", "lat", None),
        P("lat", None),
        P(),
        P(),
        P(None, "build", "lat", None),
        P(None, "build", "lat", None),
    )
    out_specs = (P(None, "build", "lat", None), P("build", "lat", None))
    return jax.shard_map(
        on_device, mesh=mesh, in_specs=in_specs, out_specs=out_specs, check_vma=False
    )
```

```python
import functools

import jax
import jax.numpy as jnp
import numpy as np
from jax import lax
from jax.experimental import pallas as pl
from jax.experimental.pallas import tpu as pltpu
from jax.sharding import PartitionSpec as P

smooth_eps = 0.0001
root_eps = 0.01
base_floor = 0.05
modulus_floor = 0.001
HALO = 8
MESH = pl.DeviceIdType.MESH
COPIES = 31
NO_KEY = 1 << 20


def lane_keys(layers, rows, first_field):
    deep = layers + 2
    inner = 3 * deep * rows
    total = inner + 2 * deep * HALO
    place = np.full((2, total), NO_KEY, np.int32)
    for k in range(total):
        if k < inner:
            place[0, k] = k // rows
            place[1, k] = k % rows
        else:
            e = k - inner
            side, z, f = e // (deep * HALO), (e // HALO) % deep, e % HALO - first_field
            if 0 <= f < 3:
                place[0, k] = f * deep + z
                place[1, k] = -1 if side == 0 else rows
    return place


def column_frames(nb, nl, ny):
    spare = 128 * (-(-nb * nl // 128))
    half = ny // 2
    if half % 128 or half <= spare:
        return [(0, ny, 0, ny)]
    return [(0, half + spare, 0, half), (half - spare, half + spare, half, ny)]


def kernel(
    nb, nlat,
    pattern, blocks, keys, den_in, smask_in, disp_in, adj_in,
    force, sens,
    den, smask, disp, adj,
    dext, rin, below, pout, pext, sext, above, cbin, pas, base, coef, gext, dz, az, es, er,
    mats, xs, prod, send_sem, recv_sem, local_sem,
):
    nl, nx, ny = den.shape
    rows = nx + 2 * HALO
    deep = nl + 2
    mid = slice(HALO, HALO + nx)
    lo = slice(0, HALO)
    hi = slice(HALO + nx, rows)
    b = lax.axis_index("build")
    l = lax.axis_index("lat")
    first_b, last_b = b == 0, b == nb - 1
    upper = b >= nb // 2

    top = nl - 1
    frames = column_frames(nb, nl, ny)
    edge = (15, 16, 26, 27)
    up = ((13, 14, 12), (24, 25, 23))
    down = ((21, 22, 20), (29, 30, 28))

    def forward_copies(f):
        start_col, width = frames[f][:2]
        cols = slice(start_col, start_col + width)
        return [
            (lambda: pout.at[f, mid], lambda: rin.at[f, mid], 1, 0),
            (lambda: pout.at[f, nx : nx + HALO], lambda: rin.at[f, lo], 1, 1),
            (lambda: pout.at[f, HALO : 2 * HALO], lambda: rin.at[f, hi], 1, -1),
            (lambda: base.at[nx - HALO : nx, cols], lambda: rin.at[f, lo], 0, 1),
            (lambda: base.at[0:HALO, cols], lambda: rin.at[f, hi], 0, -1),
        ]

    def backward_copies(f):
        return [
            (lambda: pas.at[f, 0:nx], lambda: cbin.at[f, mid], -1, 0),
            (lambda: pas.at[f, nx - HALO : nx], lambda: cbin.at[f, lo], -1, 1),
            (lambda: pas.at[f, 0:HALO], lambda: cbin.at[f, hi], -1, -1),
        ]

    table = [
        (lambda: den.at[:, nx - HALO : nx], lambda: dext.at[:, lo], 0, 1),
        (lambda: den.at[:, 0:HALO], lambda: dext.at[:, hi], 0, -1),
        (lambda: es.at[1], lambda: er.at[0, 1 : 1 + nl], 0, 1),
        (lambda: es.at[0], lambda: er.at[1, 1 : 1 + nl], 0, -1),
        (lambda: es.at[1, top], lambda: er.at[0, 0], 1, 1),
        (lambda: es.at[0, top], lambda: er.at[1, 0], 1, -1),
        (lambda: es.at[1, 0], lambda: er.at[0, nl + 1], -1, 1),
        (lambda: es.at[0, 0], lambda: er.at[1, nl + 1], -1, -1),
        (lambda: adj.at[:, top], lambda: az.at[0], 1, 0),
        (lambda: adj.at[:, 0], lambda: az.at[1], -1, 0),
        (lambda: disp.at[:, top], lambda: dz.at[0], 1, 0),
        (lambda: disp.at[:, 0], lambda: dz.at[1], -1, 0),
        *forward_copies(0),
        (lambda: pext.at[0], lambda: above, -1, 0),
        (lambda: gext.at[:, nx : nx + HALO], lambda: gext.at[:, lo], 0, 1),
        (lambda: gext.at[:, HALO : 2 * HALO], lambda: gext.at[:, hi], 0, -1),
        *backward_copies(0),
        *(forward_copies(1) if len(frames) == 2 else ()),
        *(backward_copies(1) if len(frames) == 2 else ()),
    ]

    def there(db, dl):
        ok = None
        for at, step, count in ((b, db, nb), (l, dl, nlat)):
            if step == 0:
                continue
            here = at < count - 1 if step > 0 else at > 0
            ok = here if ok is None else jnp.logical_and(ok, here)
        return ok

    def may_send(i):
        _, _, db, dl = table[i]
        ok = there(db, dl)
        return jnp.logical_and(ok, first_b) if i in edge else ok

    def may_take(i):
        _, _, db, dl = table[i]
        ok = there(-db, -dl)
        return jnp.logical_and(ok, first_b) if i in edge else ok

    def made(i):
        src, dst, db, dl = table[i]
        return pltpu.make_async_remote_copy(
            src_ref=src(), dst_ref=dst(),
            send_sem=send_sem.at[i], recv_sem=recv_sem.at[i],
            device_id=(b + db, l + dl), device_id_type=MESH,
        )

    def start(*numbers):
        for i in numbers:
            @pl.when(may_send(i))
            def _():
                made(i).start()

    def take(*numbers):
        for i in numbers:
            @pl.when(may_take(i))
            def _():
                made(i).wait_recv()

    def zero_if(cond, ref):
        @pl.when(cond)
        def _():
            ref[...] = jnp.zeros(ref.shape, jnp.float32)

    def within(width):
        row_at = l * nx - HALO + lax.broadcasted_iota(jnp.int32, (rows, width), 0)
        return jnp.logical_and(row_at >= 0, row_at < nlat * nx)

    def beside(w):
        col = lax.broadcasted_iota(jnp.int32, w.shape, 1)
        left = jnp.where(col == 0, 0.0, pltpu.roll(w, 1, 1))
        right = jnp.where(col == w.shape[1] - 1, 0.0, pltpu.roll(w, w.shape[1] - 1, 1))
        return left, right

    def cross(w):
        left, right = beside(w)
        return w + pltpu.roll(w, 1, 0) + pltpu.roll(w, rows - 1, 0) + left + right

    loads = [
        pltpu.make_async_copy(src, dst, local_sem.at[n])
        for n, (src, dst) in enumerate(
            ((den_in, den), (smask_in, smask), (adj_in, adj), (disp_in, disp))
        )
    ]
    for load in loads:
        load.start()
    barrier = pltpu.get_barrier_semaphore()
    steps = [(i, j) for i in (-1, 0, 1) for j in (-1, 0, 1) if (i, j) != (0, 0)]
    for i, j in steps:
        @pl.when(there(i, j))
        def _():
            pl.semaphore_signal(barrier, inc=1, device_id=(b + i, l + j), device_id_type=MESH)
    wide = 1 + (b > 0).astype(jnp.int32) + (b < nb - 1).astype(jnp.int32)
    tall = 1 + (l > 0).astype(jnp.int32) + (l < nlat - 1).astype(jnp.int32)
    pl.semaphore_wait(barrier, wide * tall - 1)

    loads[0].wait()
    start(0, 1)
    loads[1].wait()

    @pl.when(first_b)
    def _():
        plane = base_floor + (1.0 - base_floor) * smask[...].astype(jnp.float32)
        base[...] = plane
        for f, (start_col, width, *_) in enumerate(frames):
            rin[f, mid] = plane[:, start_col : start_col + width]

    start(*edge[: 2 * len(frames)])
    for z in range(nl):
        dext[z, mid] = den[z]
    loads[2].wait()
    loads[3].wait()
    for side, row in ((0, 0), (1, nx - 1)):
        for z in range(nl):
            for d in range(3):
                es[side, z, d : d + 1, :] = disp[d, z, row : row + 1, :]
                es[side, z, 3 + d : 4 + d, :] = adj[d, z, row : row + 1, :]
            es[side, z, 6:8, :] = jnp.zeros((2, ny), jnp.float32)
    start(2, 3, 4, 5, 6, 7, 8, 9)

    @pl.when(upper)
    def _():
        start(10, 11)

    for i in (0, 1, 2, 3, 4, 5, 6, 7, 8, 9, 10, 11, 17, 18, 19):
        _, dst, db, dl = table[i]
        zero_if(jnp.logical_not(there(-db, -dl)), dst())
    for f in range(len(frames)):
        zero_if(l == 0, rin.at[f, lo])
        zero_if(l == nlat - 1, rin.at[f, hi])
        zero_if(last_b, cbin.at[f, mid])
        zero_if(jnp.logical_or(last_b, l == 0), cbin.at[f, lo])
        zero_if(jnp.logical_or(last_b, l == nlat - 1), cbin.at[f, hi])

    def forward():
        take(0, 1)
        for f, (start_col, width, kept, until) in enumerate(frames):
            own, inner_cols = slice(kept, until), slice(kept - start_col, until - start_col)
            inside = within(width)
            take(*up[f], *edge[2 * f : 2 * f + 2])
            p = rin[f]
            for z in range(nl):
                p2 = p * p
                p4 = p2 * p2
                p8 = p4 * p4
                w = jnp.where(inside, p8 * p8, 0.0)
                total = jnp.where(inside, cross(w), 1.0)
                s = lax.rsqrt(lax.rsqrt(lax.rsqrt(lax.rsqrt(total))))
                d = dext[z, :, start_col : start_col + width]
                differ = d - s
                t = differ * differ + smooth_eps
                p = 0.5 * (d + s - t * lax.rsqrt(t) + root_eps)
                if z == top:
                    pout[f] = p
                    start(*up[f])
                pext[z, :, own] = p[:, inner_cols]
                sext[z, :, own] = s[:, inner_cols]
            below[:, own] = rin[f, :, inner_cols]
        start(17)
        inside = within(ny)
        for z in range(nl):
            p, s, d = pext[z], sext[z], dext[z]
            differ = d - s
            slope = differ * lax.rsqrt(differ * differ + smooth_eps)
            p2 = p * p
            p4 = p2 * p2
            p8 = p4 * p4
            s2 = s * s
            s4 = s2 * s2
            s8 = s4 * s4
            coef[0, z] = p8 * p4 * (p2 * p)
            coef[1, z] = jnp.where(inside, 0.5 * (1.0 + slope) / (s8 * s4 * (s2 * s)), 0.0)
            coef[2, z] = 0.5 * (1.0 - slope)
            coef[3, z] = (3.0 * (1.0 - modulus_floor)) * p2

    wide_k = keys.shape[-1]

    def build(which):
        x = lax.broadcasted_iota(jnp.int32, (nx, wide_k), 0)
        dzk = jnp.broadcast_to(keys[which, 0:1, :], (nx, wide_k))
        off = jnp.broadcast_to(keys[which, 1:2, :], (nx, wide_k)) - x + 1
        near = jnp.logical_and(off >= 0, off <= 2)
        key = jnp.where(near, dzk * 4 + off, -1)
        for z in range(nl):
            for c in range(3):
                sums = [jnp.zeros((nx, wide_k), jnp.float32) for _ in range(3)]
                for d in range(3):
                    for a in range(3):
                        for bx in range(3):
                            hit = key == (d * deep + z + a) * 4 + bx
                            for s in range(3):
                                o = 9 * a + 3 * bx + s
                                if which == 0:
                                    value = blocks[c, d, pattern[o]]
                                else:
                                    value = blocks[d, c, pattern[26 - o]]
                                sums[s] = jnp.where(hit, value, sums[s])
                for s in range(3):
                    at = ((s * 3 + c) * nl + z) * nx
                    high = sums[s].astype(jnp.bfloat16)
                    mats[0, at : at + nx, :] = high
                    mats[1, at : at + nx, :] = (sums[s] - high.astype(jnp.float32)).astype(
                        jnp.bfloat16
                    )

    def multiply():
        step = 256 if ny % 256 == 0 else 128

        def chunk(n, _):
            cols = pl.ds(pl.multiple_of(n * step, step), step)
            x = xs[:, cols]
            xh = x.astype(jnp.bfloat16)
            xl = (x - xh.astype(jnp.float32)).astype(jnp.bfloat16)
            dot = functools.partial(jnp.dot, preferred_element_type=jnp.float32)
            prod[:, cols] = dot(mats[0], xh) + (dot(mats[0], xl) + dot(mats[1], xh))
            return 0

        lax.fori_loop(0, ny // step, chunk, 0)

    def gathered(c):
        n = nl * nx
        left, _ = beside(prod[c * n : (c + 1) * n, :])
        _, right = beside(prod[(6 + c) * n : (7 + c) * n, :])
        return prod[(3 + c) * n : (4 + c) * n, :] + left + right

    inner = 3 * deep * nx

    def early():
        build(1)
        take(2, 3, 4, 5, 6, 7, 8, 9)
        for d in range(3):
            for z in range(deep):
                at = (d * deep + z) * nx
                if z == 0:
                    xs[at : at + nx, :] = az[0, d]
                elif z == deep - 1:
                    xs[at : at + nx, :] = az[1, d]
                else:
                    xs[at : at + nx, :] = adj[d, z - 1]
        for side in range(2):
            for z in range(deep):
                at = inner + (side * deep + z) * HALO
                xs[at : at + HALO, :] = er[side, z]
        multiply()
        parts = [gathered(c) for c in range(3)]
        for z in range(nl):
            g = disp[0, z] * parts[0][z * nx : (z + 1) * nx]
            g = g + disp[1, z] * parts[1][z * nx : (z + 1) * nx]
            gext[z, mid] = g + disp[2, z] * parts[2][z * nx : (z + 1) * nx]
        start(18, 19)
        build(0)

    def first(i, _):
        turn = (i == 0) == upper
        pl.when(turn)(early)
        pl.when(jnp.logical_not(turn))(forward)
        return 0

    lax.fori_loop(0, 2, first, 0)

    @pl.when(jnp.logical_not(upper))
    def _():
        start(10, 11)

    take(18, 19)
    for z in range(nl):
        coef[3, z] = coef[3, z] * gext[z]

    def stiffness():
        take(10, 11, 17)
        for z in range(deep):
            ref = below if z == 0 else (above if z == deep - 1 else pext.at[z - 1])
            p = ref[mid]
            m = modulus_floor + (1.0 - modulus_floor) * (p * p * p)
            for d in range(3):
                at = (d * deep + z) * nx
                if z == 0:
                    u = dz[0, d]
                elif z == deep - 1:
                    u = dz[1, d]
                else:
                    u = disp[d, z - 1]
                xs[at : at + nx, :] = m * u
            for side, row in ((0, HALO - 1), (1, HALO + nx)):
                at = inner + (side * deep + z) * HALO
                p = ref[row : row + 1, :]
                m = modulus_floor + (1.0 - modulus_floor) * (p * p * p)
                xs[at : at + HALO, :] = m * er[side, z]
        multiply()
        for c in range(3):
            part = gathered(c)
            for z in range(nl):
                force[c, z] = part[z * nx : (z + 1) * nx]

    def backward():
        for f, (start_col, width, kept, until) in enumerate(frames):
            cols = slice(start_col, start_col + width)
            own, inner_cols = slice(kept, until), slice(kept - start_col, until - start_col)
            take(*down[f])
            passed = cbin[f]
            for z in reversed(range(nl)):
                total = coef[3, z, :, cols] + coef[0, z, :, cols] * cross(passed)
                passed = total * coef[1, z, :, cols]
                if z == 0:
                    pas[f] = passed[mid]
                    start(*down[f])
                sens[z, :, own] = (total[:, inner_cols] * coef[2, z, :, own])[mid]

    def second(i, _):
        turn = (i == 0) == upper
        pl.when(turn)(backward)
        pl.when(jnp.logical_not(turn))(stiffness)
        return 0

    lax.fori_loop(0, 2, second, 0)

    for i in range(len(table)):
        @pl.when(may_send(i))
        def _():
            made(i).wait_send()


def on_device(density, support_mask, pattern, blocks, displacement, adjoint):
    nb, nlat = lax.axis_size("build"), lax.axis_size("lat")
    nl, nx, ny = density.shape
    rows, deep = nx + 2 * HALO, nl + 2
    keys = np.stack([lane_keys(nl, nx, 0), lane_keys(nl, nx, 3)])
    frames = column_frames(nb, nl, ny)
    count, width = len(frames), frames[0][1]
    wide_k = keys.shape[-1]
    f32 = jnp.float32
    vmem = pl.BlockSpec(memory_space=pltpu.VMEM)
    smem = pl.BlockSpec(memory_space=pltpu.SMEM)
    hbm = pl.BlockSpec(memory_space=pltpu.HBM)
    force, sens = pl.pallas_call(
        functools.partial(kernel, nb, nlat),
        out_shape=(
            jax.ShapeDtypeStruct(displacement.shape, f32),
            jax.ShapeDtypeStruct(density.shape, f32),
        ),
        in_specs=[smem, smem, vmem, hbm, hbm, hbm, hbm],
        out_specs=(vmem, vmem),
        scratch_shapes=[
            pltpu.VMEM(density.shape, f32),
            pltpu.VMEM(support_mask.shape, jnp.int32),
            pltpu.VMEM(displacement.shape, f32),
            pltpu.VMEM(adjoint.shape, f32),
            pltpu.VMEM((nl, rows, ny), f32),
            pltpu.VMEM((count, rows, width), f32),
            pltpu.VMEM((rows, ny), f32),
            pltpu.VMEM((count, rows, width), f32),
            pltpu.VMEM((nl, rows, ny), f32),
            pltpu.VMEM((nl, rows, ny), f32),
            pltpu.VMEM((rows, ny), f32),
            pltpu.VMEM((count, rows, width), f32),
            pltpu.VMEM((count, nx, width), f32),
            pltpu.VMEM((nx, ny), f32),
            pltpu.VMEM((4, nl, rows, ny), f32),
            pltpu.VMEM((nl, rows, ny), f32),
            pltpu.VMEM((2, 3, nx, ny), f32),
            pltpu.VMEM((2, 3, nx, ny), f32),
            pltpu.VMEM((2, nl, HALO, ny), f32),
            pltpu.VMEM((2, deep, HALO, ny), f32),
            pltpu.VMEM((2, 9 * nl * nx, wide_k), jnp.bfloat16),
            pltpu.VMEM((wide_k, ny), f32),
            pltpu.VMEM((9 * nl * nx, ny), f32),
            pltpu.SemaphoreType.DMA((COPIES,)),
            pltpu.SemaphoreType.DMA((COPIES,)),
            pltpu.SemaphoreType.DMA((4,)),
        ],
        compiler_params=pltpu.CompilerParams(
            collective_id=0, has_side_effects=True, vmem_limit_bytes=63 * 1024 * 1024
        ),
    )(pattern, jnp.transpose(blocks, (1, 2, 0)), jnp.asarray(keys), density, support_mask, displacement, adjoint)
    return force, sens


def solution(mesh):
    in_specs = (
        P("build", "lat", None),
        P("lat", None),
        P(),
        P(),
        P(None, "build", "lat", None),
        P(None, "build", "lat", None),
    )
    out_specs = (P(None, "build", "lat", None), P("build", "lat", None))
    return jax.shard_map(
        on_device, mesh=mesh, in_specs=in_specs, out_specs=out_specs, check_vma=False
    )
```

```python
import functools

import jax
import jax.numpy as jnp
import numpy as np
from jax import lax
from jax.experimental import pallas as pl
from jax.experimental.pallas import tpu as pltpu
from jax.sharding import PartitionSpec as P

smooth_eps = 0.0001
root_eps = 0.01
base_floor = 0.05
modulus_floor = 0.001
HALO = 8
MESH = pl.DeviceIdType.MESH
COPIES = 31
NO_KEY = 1 << 20


def lane_keys(layers, rows, first_field):
    deep = layers + 2
    inner = 3 * deep * rows
    total = inner + 2 * deep * HALO
    place = np.full((2, total), NO_KEY, np.int32)
    for k in range(total):
        if k < inner:
            place[0, k] = k // rows
            place[1, k] = k % rows
        else:
            e = k - inner
            side, z, f = e // (deep * HALO), (e // HALO) % deep, e % HALO - first_field
            if 0 <= f < 3:
                place[0, k] = f * deep + z
                place[1, k] = -1 if side == 0 else rows
    return place


def column_frames(nb, nl, ny):
    spare = 128 * (-(-nb * nl // 128))
    half = ny // 2
    if half % 128 or half <= spare:
        return [(0, ny, 0, ny)]
    return [(0, half + spare, 0, half), (half - spare, half + spare, half, ny)]


def kernel(
    nb, nlat,
    pattern, blocks, keys, den_in, smask_in, disp_in, adj_in,
    force, sens,
    den, smask, disp, adj,
    dext, rin, below, pout, pext, sext, above, cbin, pas, base, coef, gext, dz, az, es, er,
    mats, xs, prod, send_sem, recv_sem, local_sem,
):
    nl, nx, ny = den.shape
    rows = nx + 2 * HALO
    deep = nl + 2
    mid = slice(HALO, HALO + nx)
    lo = slice(0, HALO)
    hi = slice(HALO + nx, rows)
    b = lax.axis_index("build")
    l = lax.axis_index("lat")
    first_b, last_b = b == 0, b == nb - 1
    upper = b >= nb // 2

    top = nl - 1
    frames = column_frames(nb, nl, ny)
    edge = (15, 16, 26, 27)
    up = ((13, 14, 12), (24, 25, 23))
    down = ((21, 22, 20), (29, 30, 28))

    def forward_copies(f):
        start_col, width = frames[f][:2]
        cols = slice(start_col, start_col + width)
        return [
            (lambda: pout.at[f, mid], lambda: rin.at[f, mid], 1, 0),
            (lambda: pout.at[f, nx : nx + HALO], lambda: rin.at[f, lo], 1, 1),
            (lambda: pout.at[f, HALO : 2 * HALO], lambda: rin.at[f, hi], 1, -1),
            (lambda: base.at[nx - HALO : nx, cols], lambda: rin.at[f, lo], 0, 1),
            (lambda: base.at[0:HALO, cols], lambda: rin.at[f, hi], 0, -1),
        ]

    def backward_copies(f):
        return [
            (lambda: pas.at[f, 0:nx], lambda: cbin.at[f, mid], -1, 0),
            (lambda: pas.at[f, nx - HALO : nx], lambda: cbin.at[f, lo], -1, 1),
            (lambda: pas.at[f, 0:HALO], lambda: cbin.at[f, hi], -1, -1),
        ]

    table = [
        (lambda: den.at[:, nx - HALO : nx], lambda: dext.at[:, lo], 0, 1),
        (lambda: den.at[:, 0:HALO], lambda: dext.at[:, hi], 0, -1),
        (lambda: es.at[1], lambda: er.at[0, 1 : 1 + nl], 0, 1),
        (lambda: es.at[0], lambda: er.at[1, 1 : 1 + nl], 0, -1),
        (lambda: es.at[1, top], lambda: er.at[0, 0], 1, 1),
        (lambda: es.at[0, top], lambda: er.at[1, 0], 1, -1),
        (lambda: es.at[1, 0], lambda: er.at[0, nl + 1], -1, 1),
        (lambda: es.at[0, 0], lambda: er.at[1, nl + 1], -1, -1),
        (lambda: adj.at[:, top], lambda: az.at[0], 1, 0),
        (lambda: adj.at[:, 0], lambda: az.at[1], -1, 0),
        (lambda: disp.at[:, top], lambda: dz.at[0], 1, 0),
        (lambda: disp.at[:, 0], lambda: dz.at[1], -1, 0),
        *forward_copies(0),
        (lambda: pext.at[0], lambda: above, -1, 0),
        (lambda: gext.at[:, nx : nx + HALO], lambda: gext.at[:, lo], 0, 1),
        (lambda: gext.at[:, HALO : 2 * HALO], lambda: gext.at[:, hi], 0, -1),
        *backward_copies(0),
        *(forward_copies(1) if len(frames) == 2 else ()),
        *(backward_copies(1) if len(frames) == 2 else ()),
    ]

    def there(db, dl):
        ok = None
        for at, step, count in ((b, db, nb), (l, dl, nlat)):
            if step == 0:
                continue
            here = at < count - 1 if step > 0 else at > 0
            ok = here if ok is None else jnp.logical_and(ok, here)
        return ok

    def may_send(i):
        _, _, db, dl = table[i]
        ok = there(db, dl)
        return jnp.logical_and(ok, first_b) if i in edge else ok

    def may_take(i):
        _, _, db, dl = table[i]
        ok = there(-db, -dl)
        return jnp.logical_and(ok, first_b) if i in edge else ok

    def made(i):
        src, dst, db, dl = table[i]
        return pltpu.make_async_remote_copy(
            src_ref=src(), dst_ref=dst(),
            send_sem=send_sem.at[i], recv_sem=recv_sem.at[i],
            device_id=(b + db, l + dl), device_id_type=MESH,
        )

    def start(*numbers):
        for i in numbers:
            @pl.when(may_send(i))
            def _():
                made(i).start()

    def take(*numbers):
        for i in numbers:
            @pl.when(may_take(i))
            def _():
                made(i).wait_recv()

    def zero_if(cond, ref):
        @pl.when(cond)
        def _():
            ref[...] = jnp.zeros(ref.shape, jnp.float32)

    def within(width):
        row_at = l * nx - HALO + lax.broadcasted_iota(jnp.int32, (rows, width), 0)
        return jnp.logical_and(row_at >= 0, row_at < nlat * nx)

    def beside(w):
        col = lax.broadcasted_iota(jnp.int32, w.shape, 1)
        left = jnp.where(col == 0, 0.0, pltpu.roll(w, 1, 1))
        right = jnp.where(col == w.shape[1] - 1, 0.0, pltpu.roll(w, w.shape[1] - 1, 1))
        return left, right

    def cross(w):
        left, right = beside(w)
        return w + pltpu.roll(w, 1, 0) + pltpu.roll(w, rows - 1, 0) + left + right

    loads = [
        pltpu.make_async_copy(src, dst, local_sem.at[n])
        for n, (src, dst) in enumerate(
            ((den_in, den), (smask_in, smask), (adj_in, adj), (disp_in, disp))
        )
    ]
    for load in loads:
        load.start()
    barrier = pltpu.get_barrier_semaphore()
    steps = [(i, j) for i in (-1, 0, 1) for j in (-1, 0, 1) if (i, j) != (0, 0)]
    for i, j in steps:
        @pl.when(there(i, j))
        def _():
            pl.semaphore_signal(barrier, inc=1, device_id=(b + i, l + j), device_id_type=MESH)
    wide = 1 + (b > 0).astype(jnp.int32) + (b < nb - 1).astype(jnp.int32)
    tall = 1 + (l > 0).astype(jnp.int32) + (l < nlat - 1).astype(jnp.int32)
    pl.semaphore_wait(barrier, wide * tall - 1)

    loads[0].wait()
    start(0, 1)
    loads[1].wait()

    @pl.when(first_b)
    def _():
        plane = base_floor + (1.0 - base_floor) * smask[...].astype(jnp.float32)
        base[...] = plane
        for f, (start_col, width, *_) in enumerate(frames):
            rin[f, mid] = plane[:, start_col : start_col + width]

    start(*edge[: 2 * len(frames)])
    for z in range(nl):
        dext[z, mid] = den[z]
    for i in (0, 1):
        _, dst, db, dl = table[i]
        zero_if(jnp.logical_not(there(-db, -dl)), dst())
    for f in range(len(frames)):
        zero_if(l == 0, rin.at[f, lo])
        zero_if(l == nlat - 1, rin.at[f, hi])

    def forward():
        take(0, 1)
        for f, (start_col, width, kept, until) in enumerate(frames):
            own, inner_cols = slice(kept, until), slice(kept - start_col, until - start_col)
            inside = within(width)
            take(*up[f], *edge[2 * f : 2 * f + 2])
            p = rin[f]
            for z in range(nl):
                p2 = p * p
                p4 = p2 * p2
                p8 = p4 * p4
                w = jnp.where(inside, p8 * p8, 0.0)
                total = jnp.where(inside, cross(w), 1.0)
                s = lax.rsqrt(lax.rsqrt(lax.rsqrt(lax.rsqrt(total))))
                d = dext[z, :, start_col : start_col + width]
                differ = d - s
                t = differ * differ + smooth_eps
                p = 0.5 * (d + s - t * lax.rsqrt(t) + root_eps)
                if z == top:
                    pout[f] = p
                    start(*up[f])
                pext[z, :, own] = p[:, inner_cols]
                sext[z, :, own] = s[:, inner_cols]
            below[:, own] = rin[f, :, inner_cols]
        start(17)
        inside = within(ny)
        for z in range(nl):
            p, s, d = pext[z], sext[z], dext[z]
            differ = d - s
            slope = differ * lax.rsqrt(differ * differ + smooth_eps)
            p2 = p * p
            p4 = p2 * p2
            p8 = p4 * p4
            s2 = s * s
            s4 = s2 * s2
            s8 = s4 * s4
            coef[0, z] = p8 * p4 * (p2 * p)
            coef[1, z] = jnp.where(inside, 0.5 * (1.0 + slope) / (s8 * s4 * (s2 * s)), 0.0)
            coef[2, z] = 0.5 * (1.0 - slope)
            coef[3, z] = (3.0 * (1.0 - modulus_floor)) * p2

    pl.when(first_b)(forward)

    loads[2].wait()
    loads[3].wait()
    for side, row in ((0, 0), (1, nx - 1)):
        for z in range(nl):
            for d in range(3):
                es[side, z, d : d + 1, :] = disp[d, z, row : row + 1, :]
                es[side, z, 3 + d : 4 + d, :] = adj[d, z, row : row + 1, :]
            es[side, z, 6:8, :] = jnp.zeros((2, ny), jnp.float32)
    start(2, 3, 4, 5, 6, 7, 8, 9)

    @pl.when(upper)
    def _():
        start(10, 11)

    for i in (2, 3, 4, 5, 6, 7, 8, 9, 10, 11, 17, 18, 19):
        _, dst, db, dl = table[i]
        zero_if(jnp.logical_not(there(-db, -dl)), dst())
    for f in range(len(frames)):
        zero_if(last_b, cbin.at[f, mid])
        zero_if(jnp.logical_or(last_b, l == 0), cbin.at[f, lo])
        zero_if(jnp.logical_or(last_b, l == nlat - 1), cbin.at[f, hi])

    wide_k = keys.shape[-1]

    def build(which):
        x = lax.broadcasted_iota(jnp.int32, (nx, wide_k), 0)
        dzk = jnp.broadcast_to(keys[which, 0:1, :], (nx, wide_k))
        off = jnp.broadcast_to(keys[which, 1:2, :], (nx, wide_k)) - x + 1
        near = jnp.logical_and(off >= 0, off <= 2)
        key = jnp.where(near, dzk * 4 + off, -1)
        for z in range(nl):
            for c in range(3):
                sums = [jnp.zeros((nx, wide_k), jnp.float32) for _ in range(3)]
                for d in range(3):
                    for a in range(3):
                        for bx in range(3):
                            hit = key == (d * deep + z + a) * 4 + bx
                            for s in range(3):
                                o = 9 * a + 3 * bx + s
                                if which == 0:
                                    value = blocks[c, d, pattern[o]]
                                else:
                                    value = blocks[d, c, pattern[26 - o]]
                                sums[s] = jnp.where(hit, value, sums[s])
                for s in range(3):
                    at = ((s * 3 + c) * nl + z) * nx
                    high = sums[s].astype(jnp.bfloat16)
                    mats[0, at : at + nx, :] = high
                    mats[1, at : at + nx, :] = (sums[s] - high.astype(jnp.float32)).astype(
                        jnp.bfloat16
                    )

    def multiply():
        step = 256 if ny % 256 == 0 else 128

        def chunk(n, _):
            cols = pl.ds(pl.multiple_of(n * step, step), step)
            x = xs[:, cols]
            xh = x.astype(jnp.bfloat16)
            xl = (x - xh.astype(jnp.float32)).astype(jnp.bfloat16)
            dot = functools.partial(jnp.dot, preferred_element_type=jnp.float32)
            prod[:, cols] = dot(mats[0], xh) + (dot(mats[0], xl) + dot(mats[1], xh))
            return 0

        lax.fori_loop(0, ny // step, chunk, 0)

    def gathered(c):
        n = nl * nx
        left, _ = beside(prod[c * n : (c + 1) * n, :])
        _, right = beside(prod[(6 + c) * n : (7 + c) * n, :])
        return prod[(3 + c) * n : (4 + c) * n, :] + left + right

    inner = 3 * deep * nx

    def early():
        build(1)
        take(2, 3, 4, 5, 6, 7, 8, 9)
        for d in range(3):
            for z in range(deep):
                at = (d * deep + z) * nx
                if z == 0:
                    xs[at : at + nx, :] = az[0, d]
                elif z == deep - 1:
                    xs[at : at + nx, :] = az[1, d]
                else:
                    xs[at : at + nx, :] = adj[d, z - 1]
        for side in range(2):
            for z in range(deep):
                at = inner + (side * deep + z) * HALO
                xs[at : at + HALO, :] = er[side, z]
        multiply()
        parts = [gathered(c) for c in range(3)]
        for z in range(nl):
            g = disp[0, z] * parts[0][z * nx : (z + 1) * nx]
            g = g + disp[1, z] * parts[1][z * nx : (z + 1) * nx]
            gext[z, mid] = g + disp[2, z] * parts[2][z * nx : (z + 1) * nx]
        start(18, 19)
        build(0)

    def first(i, _):
        turn = (i == 0) == upper
        pl.when(turn)(early)
        pl.when(jnp.logical_not(jnp.logical_or(turn, first_b)))(forward)
        return 0

    lax.fori_loop(0, 2, first, 0)

    @pl.when(jnp.logical_not(upper))
    def _():
        start(10, 11)

    take(18, 19)
    for z in range(nl):
        coef[3, z] = coef[3, z] * gext[z]

    def stiffness():
        take(10, 11, 17)
        for z in range(deep):
            ref = below if z == 0 else (above if z == deep - 1 else pext.at[z - 1])
            p = ref[mid]
            m = modulus_floor + (1.0 - modulus_floor) * (p * p * p)
            for d in range(3):
                at = (d * deep + z) * nx
                if z == 0:
                    u = dz[0, d]
                elif z == deep - 1:
                    u = dz[1, d]
                else:
                    u = disp[d, z - 1]
                xs[at : at + nx, :] = m * u
            for side, row in ((0, HALO - 1), (1, HALO + nx)):
                at = inner + (side * deep + z) * HALO
                p = ref[row : row + 1, :]
                m = modulus_floor + (1.0 - modulus_floor) * (p * p * p)
                xs[at : at + HALO, :] = m * er[side, z]
        multiply()
        for c in range(3):
            part = gathered(c)
            for z in range(nl):
                force[c, z] = part[z * nx : (z + 1) * nx]

    def backward():
        for f, (start_col, width, kept, until) in enumerate(frames):
            cols = slice(start_col, start_col + width)
            own, inner_cols = slice(kept, until), slice(kept - start_col, until - start_col)
            take(*down[f])
            passed = cbin[f]
            for z in reversed(range(nl)):
                total = coef[3, z, :, cols] + coef[0, z, :, cols] * cross(passed)
                passed = total * coef[1, z, :, cols]
                if z == 0:
                    pas[f] = passed[mid]
                    start(*down[f])
                sens[z, :, own] = (total[:, inner_cols] * coef[2, z, :, own])[mid]

    def second(i, _):
        turn = (i == 0) == upper
        pl.when(turn)(backward)
        pl.when(jnp.logical_not(turn))(stiffness)
        return 0

    lax.fori_loop(0, 2, second, 0)

    for i in range(len(table)):
        @pl.when(may_send(i))
        def _():
            made(i).wait_send()


def on_device(density, support_mask, pattern, blocks, displacement, adjoint):
    nb, nlat = lax.axis_size("build"), lax.axis_size("lat")
    nl, nx, ny = density.shape
    rows, deep = nx + 2 * HALO, nl + 2
    keys = np.stack([lane_keys(nl, nx, 0), lane_keys(nl, nx, 3)])
    frames = column_frames(nb, nl, ny)
    count, width = len(frames), frames[0][1]
    wide_k = keys.shape[-1]
    f32 = jnp.float32
    vmem = pl.BlockSpec(memory_space=pltpu.VMEM)
    smem = pl.BlockSpec(memory_space=pltpu.SMEM)
    hbm = pl.BlockSpec(memory_space=pltpu.HBM)
    force, sens = pl.pallas_call(
        functools.partial(kernel, nb, nlat),
        out_shape=(
            jax.ShapeDtypeStruct(displacement.shape, f32),
            jax.ShapeDtypeStruct(density.shape, f32),
        ),
        in_specs=[smem, smem, vmem, hbm, hbm, hbm, hbm],
        out_specs=(vmem, vmem),
        scratch_shapes=[
            pltpu.VMEM(density.shape, f32),
            pltpu.VMEM(support_mask.shape, jnp.int32),
            pltpu.VMEM(displacement.shape, f32),
            pltpu.VMEM(adjoint.shape, f32),
            pltpu.VMEM((nl, rows, ny), f32),
            pltpu.VMEM((count, rows, width), f32),
            pltpu.VMEM((rows, ny), f32),
            pltpu.VMEM((count, rows, width), f32),
            pltpu.VMEM((nl, rows, ny), f32),
            pltpu.VMEM((nl, rows, ny), f32),
            pltpu.VMEM((rows, ny), f32),
            pltpu.VMEM((count, rows, width), f32),
            pltpu.VMEM((count, nx, width), f32),
            pltpu.VMEM((nx, ny), f32),
            pltpu.VMEM((4, nl, rows, ny), f32),
            pltpu.VMEM((nl, rows, ny), f32),
            pltpu.VMEM((2, 3, nx, ny), f32),
            pltpu.VMEM((2, 3, nx, ny), f32),
            pltpu.VMEM((2, nl, HALO, ny), f32),
            pltpu.VMEM((2, deep, HALO, ny), f32),
            pltpu.VMEM((2, 9 * nl * nx, wide_k), jnp.bfloat16),
            pltpu.VMEM((wide_k, ny), f32),
            pltpu.VMEM((9 * nl * nx, ny), f32),
            pltpu.SemaphoreType.DMA((COPIES,)),
            pltpu.SemaphoreType.DMA((COPIES,)),
            pltpu.SemaphoreType.DMA((4,)),
        ],
        compiler_params=pltpu.CompilerParams(
            collective_id=0, has_side_effects=True, vmem_limit_bytes=63 * 1024 * 1024
        ),
    )(pattern, jnp.transpose(blocks, (1, 2, 0)), jnp.asarray(keys), density, support_mask, displacement, adjoint)
    return force, sens


def solution(mesh):
    in_specs = (
        P("build", "lat", None),
        P("lat", None),
        P(),
        P(),
        P(None, "build", "lat", None),
        P(None, "build", "lat", None),
    )
    out_specs = (P(None, "build", "lat", None), P("build", "lat", None))
    return jax.shard_map(
        on_device, mesh=mesh, in_specs=in_specs, out_specs=out_specs, check_vma=False
    )
```
